32 devices in a mesh: groups: 2 (over y), row: 4 (over z), col: 4 (over x, core).
Axes of the slice: x: 2, y: 2, z: 4, core: 2. Of those that a mesh axis runs over, the one named last changes fastest.
Arguments:
- grad_out: bfloat16 [2048, 12288], P(('groups', 'row'), 'col'), parts along dimension 0, may hold values from -6 to 6
- preact: bfloat16 [2048, 24576], P(('groups', 'col'), 'row'), parts along dimension 0, may hold values from -6 to 6
- down_weight: bfloat16 [24576, 12288], P('row', 'col'), may hold values from -0.0546875 to 0.0546875
- sketch_matrix: bfloat16 [24576, 512], P('row'), may hold values from -0.0017089844 to 0.0017089844
Outputs:
- grad_pre: bfloat16 [2048, 24576], P(('groups', 'col'), 'row'), parts along dimension 0
- sketch: float32 [1024, 12288], P(('groups', 'row'), 'col'), parts along dimension 0
The draws below stay inside these ranges and needn't reach their ends.
There are 2 independent parts, one for each index of `groups`. The reference program is written for one: setup_inputs(seed, part) draws one part's arguments, and reference() takes and returns one part's arrays. A program takes and returns all parts, laid end to end along the dimension named above; an argument that names none is the same for every part. Nothing has to cross between parts.
All inputs are finite; a program needn't handle non-finite values.
Results may differ from the reference program's by a relative error of at most 0.011.
Values may be sent and summed in bfloat16 or wider, within the bound.
A program may use at most 192 MiB of HBM per device.

```python
import jax
import jax.numpy as jnp
from jax import lax

D = 12288
FF = 24576
R = 512
TOKENS = 1024
N_ROW = 4
N_COL = 4


def strengthened(values, key, source, target, parts, factor):
    owner, partner = [(jnp.arange(values.shape[dim]) // (values.shape[dim] // parts)).reshape([-1 if axis == dim else 1 for axis in range(values.ndim)]) for dim in (source, target)]
    chosen = jax.random.permutation(key, parts)[partner]
    strong = (owner == chosen) | (owner == (partner + parts // 2) % parts)
    return jnp.where(strong, factor * values, values)


def level_of(key, dims, cuts, least, largest):
    level, own = 1.0, jax.random.fold_in(key, 6)
    for dim, shards_of in cuts:
        heights = jnp.exp(jax.random.uniform(jax.random.fold_in(own, dim), (shards_of,), jnp.float32, least / len(cuts), largest / len(cuts)))
        level = level * jnp.repeat(heights, dims[dim] // shards_of).reshape([-1 if axis == dim else 1 for axis in range(len(dims))])
    return level


def noise(rng, dims, width, limit, pieces=(), kind=jnp.bfloat16):
    level = level_of(rng, dims, pieces, -0.22, 0.18) if pieces else 1.0
    drawn = jax.random.normal(rng, dims, jnp.float32) * width * level
    return jnp.minimum(jnp.maximum(drawn, -limit), limit).astype(kind)


def bell_draw_with(key, dims, width, limit, pieces, heavy, kind=jnp.bfloat16):
    values = width * jax.random.normal(key, dims, jnp.float32)
    if pieces:
        values = values * level_of(key, dims, pieces, -0.22, 0.18)
    return jnp.clip(strengthened(values, jax.random.fold_in(key, 3), *heavy), -limit, limit).astype(kind)


def setup_inputs(seed: int = 0, part: int = 0) -> dict:
    seeds = jax.random.split(jax.random.key(seed), 5)
    part_keys = jax.random.split(jax.random.fold_in(seeds[4], part), 5)
    return {
        "grad_out": bell_draw_with(part_keys[0], (TOKENS, D), 1.0, 6.0, ((0, 4), (1, 4)), (1, 0, 4, 2.0)),
        "preact": noise(part_keys[1], (TOKENS, FF), 1.0, 6.0, ((0, 4), (1, 4))),
        "down_weight": noise(seeds[2], (FF, D), D ** -0.5, 0.0546875, ((0, 4), (1, 4))),
        "sketch_matrix": bell_draw_with(seeds[3], (FF, R), (FF * TOKENS) ** -0.5, 0.0017089844, ((0, 4),), (0, 1, 4, 2.0)),
    }


gelu_scale = 0.7978845608028654
cubic_term = 0.044715


def gelu_parts(preact):
    pre_f32 = preact.astype(jnp.float32)
    inner_arg = gelu_scale * (pre_f32 + cubic_term * pre_f32 * pre_f32 * pre_f32)
    tangent = jnp.tanh(inner_arg)
    value = 0.5 * pre_f32 * (1.0 + tangent)
    slope = 0.5 * (1.0 + tangent) + 0.5 * pre_f32 * (1.0 - tangent * tangent) * gelu_scale * (1.0 + 3.0 * cubic_term * pre_f32 * pre_f32)
    return value, slope


def reference(grad_out, preact, down_weight, sketch_matrix):
    col_width = D // N_COL
    hidden_grad = jnp.zeros((TOKENS, FF), jnp.float32)
    for block_index in range(N_COL):
        lower = block_index * col_width
        partial_value = jnp.dot(grad_out[:, lower:lower + col_width], down_weight[:, lower:lower + col_width].T, preferred_element_type=jnp.float32)
        partial_value = lax.optimization_barrier(partial_value.astype(jnp.bfloat16)).astype(jnp.float32)
        hidden_grad = hidden_grad + partial_value
    value, slope = gelu_parts(preact)
    grad_pre = (hidden_grad * slope).astype(jnp.bfloat16)
    act = value.astype(jnp.bfloat16)
    row_count = FF // N_ROW

    def add_block(running, block_index):
        act_block = lax.dynamic_slice_in_dim(act, block_index * row_count, row_count, 1)
        omega_block = lax.dynamic_slice_in_dim(sketch_matrix, block_index * row_count, row_count, 0).astype(jnp.float32)
        grad_block = jnp.dot(act_block.T, grad_out, preferred_element_type=jnp.float32)
        running = running + jnp.dot(omega_block.T, grad_block, precision=lax.Precision.HIGHEST, preferred_element_type=jnp.float32)
        return running, None

    sketch, unused = lax.scan(add_block, jnp.zeros((R, D), jnp.float32), jnp.arange(N_ROW, dtype=jnp.int32))
    return grad_pre, sketch
```

```python
import jax
import jax.numpy as jnp
from jax import lax
from jax.sharding import PartitionSpec as P

gelu_scale = 0.7978845608028654
cubic_term = 0.044715


def gelu_parts(preact):
    pre_f32 = preact.astype(jnp.float32)
    inner_arg = gelu_scale * (pre_f32 + cubic_term * pre_f32 * pre_f32 * pre_f32)
    tangent = jnp.tanh(inner_arg)
    value = 0.5 * pre_f32 * (1.0 + tangent)
    slope = 0.5 * (1.0 + tangent) + 0.5 * pre_f32 * (1.0 - tangent * tangent) * gelu_scale * (
        1.0 + 3.0 * cubic_term * pre_f32 * pre_f32
    )
    return (value, slope)


def per_device(grad_out, preact, down_weight, sketch_matrix):
    grad_rows = lax.all_gather(grad_out, "row", axis=0, tiled=True)
    value, slope = gelu_parts(preact)
    act_local = value.astype(jnp.bfloat16)
    own = lax.dot_general(
        sketch_matrix, act_local, (((0,), (1,)), ((), ())), preferred_element_type=jnp.float32
    )
    reduced = lax.psum_scatter(own, "row", scatter_dimension=0, tiled=True)
    reduced = lax.all_gather(reduced.astype(jnp.bfloat16), "col", axis=1, tiled=True)
    hidden_grad = lax.psum_scatter(
        lax.dot_general(
            grad_rows, down_weight, (((1,), (1,)), ((), ())), preferred_element_type=jnp.float32
        ).astype(jnp.bfloat16),
        "col",
        scatter_dimension=0,
        tiled=True,
    ).astype(jnp.float32)
    grad_pre = (hidden_grad * slope).astype(jnp.bfloat16)
    sketch = jnp.dot(reduced, grad_rows, preferred_element_type=jnp.float32)
    return (grad_pre, sketch)


def solution(mesh):
    in_specs = (
        P(("groups", "row"), "col"),
        P(("groups", "col"), "row"),
        P("row", "col"),
        P("row", None),
    )
    out_specs = (P(("groups", "col"), "row"), P(("groups", "row"), "col"))
    return jax.shard_map(
        per_device, mesh=mesh, in_specs=in_specs, out_specs=out_specs, check_vma=False
    )
```

```python
import jax
import jax.numpy as jnp
from jax import lax
from jax.experimental import pallas as pl
from jax.experimental.pallas import tpu as pltpu
from jax.sharding import PartitionSpec as P

gelu_scale = 0.7978845608028654
cubic_term = 0.044715


def gelu_parts(preact):
    pre_f32 = preact.astype(jnp.float32)
    inner_arg = gelu_scale * (pre_f32 + cubic_term * pre_f32 * pre_f32 * pre_f32)
    tangent = jnp.tanh(inner_arg)
    value = 0.5 * pre_f32 * (1.0 + tangent)
    slope = 0.5 * (1.0 + tangent) + 0.5 * pre_f32 * (1.0 - tangent * tangent) * gelu_scale * (
        1.0 + 3.0 * cubic_term * pre_f32 * pre_f32
    )
    return (value, slope)


def per_device(grad_out, preact, down_weight, sketch_matrix):
    grad_rows = lax.all_gather(grad_out, "row", axis=0, tiled=True)
    value, slope = gelu_parts(preact)
    act_local = value.astype(jnp.bfloat16)
    own = lax.dot_general(
        sketch_matrix, act_local, (((0,), (1,)), ((), ())), preferred_element_type=jnp.float32
    )
    reduced = lax.psum_scatter(own, "row", scatter_dimension=0, tiled=True)
    reduced = lax.all_gather(reduced.astype(jnp.bfloat16), "col", axis=1, tiled=True)
    hidden_grad = lax.psum_scatter(
        lax.dot_general(
            grad_rows, down_weight, (((1,), (1,)), ((), ())), preferred_element_type=jnp.float32
        ).astype(jnp.bfloat16),
        "col",
        scatter_dimension=0,
        tiled=True,
    ).astype(jnp.float32)
    grad_pre = (hidden_grad * slope).astype(jnp.bfloat16)
    sketch = jnp.dot(reduced, grad_rows, preferred_element_type=jnp.float32)
    return (grad_pre, sketch)


MESH = pl.DeviceIdType.MESH
LINE = 4
TILES = 6


def fits(mesh):
    return mesh.shape["row"] == LINE and mesh.shape["col"] == LINE


def pick(index, options):
    chosen = options[0]
    for place, option in enumerate(options[1:], 1):
        chosen = jnp.where(index == place, option, chosen)
    return chosen


def encoded(pieces):
    code = 0
    for piece in reversed(pieces):
        code = code * 8 + piece
    return code


def arrival_orders():
    orders = []
    for place in range(LINE):
        order = [2 * place, 2 * place + 1]
        for distance in range(1, LINE):
            for half in range(2):
                for other in (place - distance, place + distance):
                    if 0 <= other < LINE:
                        order.append(2 * other + half)
        orders.append(encoded(order))
    return orders


def kernel(
    g_ref, w_ref, slope_ref, out_ref, rows_ref,
    wbuf, gbuf, pbuf, near, far, sums, slopes,
    w_sem, g_sem, own_sem, slope_sem, out_sem, right_sem, left_sem, got_sem,
    near_send, near_got, far_send, far_got, sum_send, sum_got,
):
    z = lax.axis_index("row")
    c = lax.axis_index("col")
    par = lax.rem(c, 2)
    other = 1 - par
    partner = c + 1 - 2 * par
    chip = lax.div(c, 2)
    has_left, has_right = z > 0, z < LINE - 1
    piece_rows = gbuf.shape[0]
    tile = wbuf.shape[2]
    half_width = tile * TILES

    def w_copy(half, j):
        start = pl.multiple_of((half * TILES + j) * tile, tile)
        return pltpu.make_async_copy(w_ref.at[pl.ds(start, tile)], wbuf.at[half, j], w_sem.at[half, j])

    def slope_copy(h, half):
        return pltpu.make_async_copy(
            slope_ref.at[pl.ds(h * piece_rows, piece_rows), pl.ds(half * half_width, half_width)],
            slopes.at[h, half],
            slope_sem.at[h, half],
        )

    def out_copy(h, half):
        return pltpu.make_async_copy(
            pbuf.at[2 * c + h, half],
            out_ref.at[pl.ds(h * piece_rows, piece_rows), pl.ds(half * half_width, half_width)],
            out_sem.at[h, half],
        )

    def rows_of(piece):
        return rows_ref.at[pl.ds(pl.multiple_of(piece * piece_rows, piece_rows), piece_rows)]

    def own_copy():
        return pltpu.make_async_copy(
            g_ref, rows_ref.at[pl.ds(pl.multiple_of(z * 2 * piece_rows, 2 * piece_rows), 2 * piece_rows)], own_sem
        )

    def pass_on(piece, step, sem, source):
        return pltpu.make_async_remote_copy(
            src_ref=source, dst_ref=rows_of(piece), send_sem=sem.at[piece], recv_sem=got_sem.at[piece],
            device_id={"row": z + step}, device_id_type=MESH,
        )

    def near_copy(piece, h, half):
        return pltpu.make_async_remote_copy(
            src_ref=pbuf.at[piece, half], dst_ref=near.at[h, half],
            send_sem=near_send.at[h, half], recv_sem=near_got.at[h, half],
            device_id={"col": partner}, device_id_type=MESH,
        )

    def far_copy(piece, index):
        return pltpu.make_async_remote_copy(
            src_ref=pbuf.at[piece, other], dst_ref=far.at[index],
            send_sem=far_send.at[index], recv_sem=far_got.at[index],
            device_id={"col": partner}, device_id_type=MESH,
        )

    def sum_copy(piece, owner, h, half, index):
        return pltpu.make_async_remote_copy(
            src_ref=pbuf.at[piece, half], dst_ref=sums.at[h, half],
            send_sem=sum_send.at[index], recv_sem=sum_got.at[h, half],
            device_id={"col": owner}, device_id_type=MESH,
        )

    own_copy().start()

    @pl.loop(0, TILES)
    def _(j):
        w_copy(other, j).start()

    barrier = pltpu.get_barrier_semaphore()
    for step in range(1, LINE):
        pl.semaphore_signal(barrier, inc=1, device_id={"col": lax.rem(c + step, LINE)}, device_id_type=MESH)

    @pl.when(has_left)
    def _():
        pl.semaphore_signal(barrier, inc=1, device_id={"row": z - 1}, device_id_type=MESH)

    @pl.when(has_right)
    def _():
        pl.semaphore_signal(barrier, inc=1, device_id={"row": z + 1}, device_id_type=MESH)

    pl.semaphore_wait(barrier, LINE - 1 + jnp.where(has_left, 1, 0) + jnp.where(has_right, 1, 0))

    for h in range(2):
        source = g_ref.at[pl.ds(h * piece_rows, piece_rows)]

        @pl.when(has_left)
        def _():
            pass_on(2 * z + h, -1, left_sem, source).start()

        @pl.when(has_right)
        def _():
            pass_on(2 * z + h, 1, right_sem, source).start()

    @pl.loop(0, TILES)
    def _(j):
        w_copy(par, j).start()

    for h in range(2):
        for half in range(2):
            slope_copy(h, half).start()
    own_copy().wait()

    def step_of(s, code):
        piece = lax.rem(code, 8)
        owner = lax.div(piece, 2)
        h = lax.rem(piece, 2)
        is_near = owner == partner
        is_far = lax.div(owner, 2) != chip
        index = 2 * lax.rem(owner, 2) + h

        @pl.when(owner != z)
        def _():
            pass_on(piece, 0, left_sem, rows_of(piece)).wait_recv()

        @pl.when((owner < z) & has_right)
        def _():
            pass_on(piece, 1, right_sem, rows_of(piece)).start()

        @pl.when((owner > z) & has_left)
        def _():
            pass_on(piece, -1, left_sem, rows_of(piece)).start()

        load = pltpu.make_async_copy(rows_of(piece), gbuf, g_sem)
        load.start()
        load.wait()

        def multiply(half):
            @pl.loop(0, TILES)
            def _(j):
                @pl.when(s == 0)
                def _():
                    w_copy(half, j).wait()

                product = lax.dot_general(
                    gbuf[...], wbuf[half, j], (((1,), (1,)), ((), ())), preferred_element_type=jnp.float32
                )
                pbuf[piece, half, :, pl.ds(pl.multiple_of(j * tile, tile), tile)] = product.astype(jnp.bfloat16)

        multiply(other)

        @pl.when(is_near)
        def _():
            near_copy(piece, h, other).start()

        @pl.when(is_far)
        def _():
            far_copy(piece, index).start()

        multiply(par)

        @pl.when(is_near)
        def _():
            near_copy(piece, h, par).start()

        @pl.when(is_far)
        def _():
            far_copy(piece, index).wait_recv()

            @pl.loop(0, TILES)
            def _(j):
                columns = pl.ds(pl.multiple_of(j * tile, tile), tile)
                total = pbuf[piece, par, :, columns].astype(jnp.float32) + far[index, :, columns].astype(jnp.float32)
                pbuf[piece, par, :, columns] = total.astype(jnp.bfloat16)

            sum_copy(piece, owner, h, par, index).start()

        return lax.div(code, 8)

    lax.fori_loop(0, 2 * LINE, step_of, pick(z, arrival_orders()))

    for h in range(2):
        for half in range(2):
            near_copy(2 * partner + h, h, half).wait_recv()
            slope_copy(h, half).wait()
            sum_copy(2 * c + h, lax.rem(c + 2, LINE), h, half, h).wait_recv()

            @pl.loop(0, TILES)
            def _(j):
                columns = pl.ds(pl.multiple_of(j * tile, tile), tile)
                hidden = (
                    pbuf[2 * c + h, half, :, columns].astype(jnp.float32)
                    + near[h, half, :, columns].astype(jnp.float32)
                    + sums[h, half, :, columns].astype(jnp.float32)
                )
                scaled = hidden * slopes[h, half, :, columns].astype(jnp.float32)
                pbuf[2 * c + h, half, :, columns] = scaled.astype(jnp.bfloat16)

            out_copy(h, half).start()

    def drain(piece, carry):
        owner = lax.div(piece, 2)
        h = lax.rem(piece, 2)
        index = 2 * lax.rem(owner, 2) + h

        @pl.when((owner <= z) & has_right)
        def _():
            pass_on(piece, 1, right_sem, rows_of(piece)).wait_send()

        @pl.when((owner >= z) & has_left)
        def _():
            pass_on(piece, -1, left_sem, rows_of(piece)).wait_send()

        @pl.when(owner == partner)
        def _():
            near_copy(piece, h, other).wait_send()
            near_copy(piece, h, par).wait_send()

        @pl.when(lax.div(owner, 2) != chip)
        def _():
            far_copy(piece, index).wait_send()
            sum_copy(piece, owner, h, par, index).wait_send()

        return carry

    lax.fori_loop(0, 2 * LINE, drain, 0)
    for h in range(2):
        for half in range(2):
            out_copy(h, half).wait()


def gathered_product(grad_out, down_weight, slope):
    tokens, features = grad_out.shape
    hidden = down_weight.shape[0]
    rows, width = tokens // 2, hidden // 2
    kind = grad_out.dtype
    pair = pltpu.SemaphoreType.DMA((2, 2))
    eight = pltpu.SemaphoreType.DMA((2 * LINE,))
    four = pltpu.SemaphoreType.DMA((4,))
    one = pltpu.SemaphoreType.DMA
    return pl.pallas_call(
        kernel,
        out_shape=(
            jax.ShapeDtypeStruct((tokens, hidden), kind),
            jax.ShapeDtypeStruct((tokens * LINE, features), kind),
        ),
        in_specs=[pl.BlockSpec(memory_space=pltpu.HBM)] * 3,
        out_specs=(pl.BlockSpec(memory_space=pltpu.HBM),) * 2,
        scratch_shapes=[
            pltpu.VMEM((2, TILES, width // TILES, features), kind),
            pltpu.VMEM((rows, features), kind),
            pltpu.VMEM((2 * LINE, 2, rows, width), kind),
            pltpu.VMEM((2, 2, rows, width), kind),
            pltpu.VMEM((4, rows, width), kind),
            pltpu.VMEM((2, 2, rows, width), kind),
            pltpu.VMEM((2, 2, rows, width), kind),
            pltpu.SemaphoreType.DMA((2, TILES)),
            one, one, pair, pair, eight, eight, eight,
            pair, pair, four, four, four, pair,
        ],
        compiler_params=pltpu.CompilerParams(
            collective_id=0, has_side_effects=True, vmem_limit_bytes=63 * 1024 * 1024
        ),
        cost_estimate=pl.CostEstimate(
            flops=2 * LINE * tokens * hidden * features * 3,
            bytes_accessed=2 * (hidden * features + 12 * tokens * features),
            transcendentals=0,
        ),
    )(grad_out, down_weight, slope)


def fused_device(grad_out, preact, down_weight, sketch_matrix):
    value, slope = gelu_parts(preact)
    grad_pre, grad_rows = gathered_product(grad_out, down_weight, slope.astype(jnp.bfloat16))
    own = lax.dot_general(
        sketch_matrix, value.astype(jnp.bfloat16), (((0,), (1,)), ((), ())), preferred_element_type=jnp.float32
    )
    reduced = lax.psum_scatter(own.astype(jnp.bfloat16), "row", scatter_dimension=0, tiled=True)
    reduced = lax.all_gather(reduced.astype(jnp.bfloat16), "col", axis=1, tiled=True)
    sketch = jnp.dot(reduced, grad_rows, preferred_element_type=jnp.float32)
    return (grad_pre, sketch)


def solution(mesh):
    body = fused_device if fits(mesh) else per_device
    in_specs = (
        P(("groups", "row"), "col"),
        P(("groups", "col"), "row"),
        P("row", "col"),
        P("row", None),
    )
    out_specs = (P(("groups", "col"), "row"), P(("groups", "row"), "col"))
    return jax.shard_map(
        body, mesh=mesh, in_specs=in_specs, out_specs=out_specs, check_vma=False
    )
```

```python
import jax
import jax.numpy as jnp
from jax import lax
from jax.experimental import pallas as pl
from jax.experimental.pallas import tpu as pltpu
from jax.sharding import PartitionSpec as P

gelu_scale = 0.7978845608028654
cubic_term = 0.044715


def gelu_parts(preact):
    pre_f32 = preact.astype(jnp.float32)
    inner_arg = gelu_scale * (pre_f32 + cubic_term * pre_f32 * pre_f32 * pre_f32)
    tangent = jnp.tanh(inner_arg)
    value = 0.5 * pre_f32 * (1.0 + tangent)
    slope = 0.5 * (1.0 + tangent) + 0.5 * pre_f32 * (1.0 - tangent * tangent) * gelu_scale * (
        1.0 + 3.0 * cubic_term * pre_f32 * pre_f32
    )
    return (value, slope)


def per_device(grad_out, preact, down_weight, sketch_matrix):
    grad_rows = lax.all_gather(grad_out, "row", axis=0, tiled=True)
    value, slope = gelu_parts(preact)
    act_local = value.astype(jnp.bfloat16)
    own = lax.dot_general(
        sketch_matrix, act_local, (((0,), (1,)), ((), ())), preferred_element_type=jnp.float32
    )
    reduced = lax.psum_scatter(own, "row", scatter_dimension=0, tiled=True)
    reduced = lax.all_gather(reduced.astype(jnp.bfloat16), "col", axis=1, tiled=True)
    hidden_grad = lax.psum_scatter(
        lax.dot_general(
            grad_rows, down_weight, (((1,), (1,)), ((), ())), preferred_element_type=jnp.float32
        ).astype(jnp.bfloat16),
        "col",
        scatter_dimension=0,
        tiled=True,
    ).astype(jnp.float32)
    grad_pre = (hidden_grad * slope).astype(jnp.bfloat16)
    sketch = jnp.dot(reduced, grad_rows, preferred_element_type=jnp.float32)
    return (grad_pre, sketch)


MESH = pl.DeviceIdType.MESH
LINE = 4
TILES = 3


def fits(mesh):
    return mesh.shape["row"] == LINE and mesh.shape["col"] == LINE


def pick(index, options):
    chosen = options[0]
    for place, option in enumerate(options[1:], 1):
        chosen = jnp.where(index == place, option, chosen)
    return chosen


def arrival_orders():
    codes = []
    for place in range(LINE):
        order = sorted(range(LINE), key=lambda block: (abs(block - place), block))
        codes.append(sum(block * LINE**position for position, block in enumerate(order)))
    return codes


def kernel(
    g_ref, w_ref, slope_ref, out_ref, rows_ref,
    wbuf, gbuf, pbuf, near, far, sums,
    w_sem, g_sem, own_sem, slope_sem, out_sem, right_sem, left_sem, got_sem,
    near_send, near_got, far_send, far_got, sum_send, sum_got,
):
    z = lax.axis_index("row")
    c = lax.axis_index("col")
    par = lax.rem(c, 2)
    other = 1 - par
    partner = c + 1 - 2 * par
    chip = lax.div(c, 2)
    has_left, has_right = z > 0, z < LINE - 1
    piece_rows = gbuf.shape[0] // 2
    tile = wbuf.shape[2]
    half_width = tile * TILES

    def w_copy(half, j):
        start = pl.multiple_of((half * TILES + j) * tile, tile)
        return pltpu.make_async_copy(w_ref.at[pl.ds(start, tile)], wbuf.at[half, j], w_sem.at[half, j])

    def slope_copy(h, half):
        return pltpu.make_async_copy(
            slope_ref.at[pl.ds(h * piece_rows, piece_rows), pl.ds(half * half_width, half_width)],
            far.at[2 * h + half],
            slope_sem.at[h, half],
        )

    def out_copy(h, half):
        return pltpu.make_async_copy(
            pbuf.at[2 * c + h, half],
            out_ref.at[pl.ds(h * piece_rows, piece_rows), pl.ds(half * half_width, half_width)],
            out_sem.at[h, half],
        )

    def rows_of(piece):
        return rows_ref.at[pl.ds(pl.multiple_of(piece * piece_rows, piece_rows), piece_rows)]

    def own_copy():
        return pltpu.make_async_copy(
            g_ref, rows_ref.at[pl.ds(pl.multiple_of(z * 2 * piece_rows, 2 * piece_rows), 2 * piece_rows)], own_sem
        )

    def pass_on(piece, step, sem, source):
        return pltpu.make_async_remote_copy(
            src_ref=source, dst_ref=rows_of(piece), send_sem=sem.at[piece], recv_sem=got_sem.at[piece],
            device_id={"row": z + step}, device_id_type=MESH,
        )

    def near_copy(piece, h, half):
        return pltpu.make_async_remote_copy(
            src_ref=pbuf.at[piece, half], dst_ref=near.at[h, half],
            send_sem=near_send.at[h, half], recv_sem=near_got.at[h, half],
            device_id={"col": partner}, device_id_type=MESH,
        )

    def far_copy(piece, index):
        return pltpu.make_async_remote_copy(
            src_ref=pbuf.at[piece, other], dst_ref=far.at[index],
            send_sem=far_send.at[index], recv_sem=far_got.at[index],
            device_id={"col": partner}, device_id_type=MESH,
        )

    def sum_copy(piece, owner, h, half, index):
        return pltpu.make_async_remote_copy(
            src_ref=pbuf.at[piece, half], dst_ref=sums.at[h, half],
            send_sem=sum_send.at[index], recv_sem=sum_got.at[h, half],
            device_id={"col": owner}, device_id_type=MESH,
        )

    own_copy().start()

    @pl.loop(0, TILES)
    def _(j):
        w_copy(other, j).start()

    barrier = pltpu.get_barrier_semaphore()
    for step in range(1, LINE):
        pl.semaphore_signal(barrier, inc=1, device_id={"col": lax.rem(c + step, LINE)}, device_id_type=MESH)

    @pl.when(has_left)
    def _():
        pl.semaphore_signal(barrier, inc=1, device_id={"row": z - 1}, device_id_type=MESH)

    @pl.when(has_right)
    def _():
        pl.semaphore_signal(barrier, inc=1, device_id={"row": z + 1}, device_id_type=MESH)

    pl.semaphore_wait(barrier, LINE - 1 + jnp.where(has_left, 1, 0) + jnp.where(has_right, 1, 0))

    for h in range(2):
        source = g_ref.at[pl.ds(h * piece_rows, piece_rows)]

        @pl.when(has_left)
        def _():
            pass_on(2 * z + h, -1, left_sem, source).start()

        @pl.when(has_right)
        def _():
            pass_on(2 * z + h, 1, right_sem, source).start()

    @pl.loop(0, TILES)
    def _(j):
        w_copy(par, j).start()

    own_copy().wait()

    def receive(block):
        for h in range(2):
            piece = 2 * block + h
            pass_on(piece, 0, left_sem, rows_of(piece)).wait_recv()

            @pl.when((block < z) & has_right)
            def _():
                pass_on(piece, 1, right_sem, rows_of(piece)).start()

            @pl.when((block > z) & has_left)
            def _():
                pass_on(piece, -1, left_sem, rows_of(piece)).start()

    middle = has_left & has_right

    def step_of(s, code):
        owner = lax.rem(code, LINE)
        later = lax.rem(lax.div(code, LINE), LINE)
        is_near = owner == partner
        is_far = lax.div(owner, 2) != chip
        first = 2 * lax.rem(owner, 2)

        @pl.when((s > 0) & ((s != 2) | jnp.logical_not(middle)))
        def _():
            receive(owner)

        @pl.when((s == 1) & middle)
        def _():
            receive(later)

        start = pl.multiple_of(owner * 2 * piece_rows, 2 * piece_rows)
        load = pltpu.make_async_copy(rows_ref.at[pl.ds(start, 2 * piece_rows)], gbuf, g_sem)
        load.start()
        load.wait()

        def multiply(half):
            @pl.loop(0, TILES)
            def _(j):
                @pl.when(s == 0)
                def _():
                    w_copy(half, j).wait()

                product = lax.dot_general(
                    gbuf[...], wbuf[half, j], (((1,), (1,)), ((), ())), preferred_element_type=jnp.float32
                ).astype(jnp.bfloat16)
                columns = pl.ds(pl.multiple_of(j * tile, tile), tile)
                for h in range(2):
                    pbuf[2 * owner + h, half, :, columns] = product[h * piece_rows : (h + 1) * piece_rows]

        multiply(other)

        @pl.when(is_near)
        def _():
            for h in range(2):
                near_copy(2 * owner + h, h, other).start()

        @pl.when(is_far)
        def _():
            for h in range(2):
                far_copy(2 * owner + h, first + h).start()

        multiply(par)

        @pl.when(is_near)
        def _():
            for h in range(2):
                near_copy(2 * owner + h, h, par).start()

        @pl.when(is_far)
        def _():
            for h in range(2):
                piece, index = 2 * owner + h, first + h
                far_copy(piece, index).wait_recv()

                @pl.loop(0, TILES)
                def _(j):
                    columns = pl.ds(pl.multiple_of(j * tile, tile), tile)
                    total = pbuf[piece, par, :, columns].astype(jnp.float32) + far[index, :, columns].astype(
                        jnp.float32
                    )
                    pbuf[piece, par, :, columns] = total.astype(jnp.bfloat16)

                sum_copy(piece, owner, h, par, index).start()

        return lax.div(code, LINE)

    lax.fori_loop(0, LINE, step_of, pick(z, arrival_orders()))

    for h in range(2):
        for half in range(2):
            slope_copy(h, half).start()

    for h in range(2):
        for half in range(2):
            near_copy(2 * partner + h, h, half).wait_recv()
            slope_copy(h, half).wait()
            sum_copy(2 * c + h, lax.rem(c + 2, LINE), h, half, h).wait_recv()

            @pl.loop(0, TILES)
            def _(j):
                columns = pl.ds(pl.multiple_of(j * tile, tile), tile)
                hidden = (
                    pbuf[2 * c + h, half, :, columns].astype(jnp.float32)
                    + near[h, half, :, columns].astype(jnp.float32)
                    + sums[h, half, :, columns].astype(jnp.float32)
                )
                scaled = hidden * far[2 * h + half, :, columns].astype(jnp.float32)
                pbuf[2 * c + h, half, :, columns] = scaled.astype(jnp.bfloat16)

            out_copy(h, half).start()

    def drain(piece, carry):
        owner = lax.div(piece, 2)
        h = lax.rem(piece, 2)
        index = 2 * lax.rem(owner, 2) + h

        @pl.when((owner <= z) & has_right)
        def _():
            pass_on(piece, 1, right_sem, rows_of(piece)).wait_send()

        @pl.when((owner >= z) & has_left)
        def _():
            pass_on(piece, -1, left_sem, rows_of(piece)).wait_send()

        @pl.when(owner == partner)
        def _():
            near_copy(piece, h, other).wait_send()
            near_copy(piece, h, par).wait_send()

        @pl.when(lax.div(owner, 2) != chip)
        def _():
            far_copy(piece, index).wait_send()
            sum_copy(piece, owner, h, par, index).wait_send()

        return carry

    lax.fori_loop(0, 2 * LINE, drain, 0)
    for h in range(2):
        for half in range(2):
            out_copy(h, half).wait()


def gathered_product(grad_out, down_weight, slope):
    tokens, features = grad_out.shape
    hidden = down_weight.shape[0]
    rows, width = tokens // 2, hidden // 2
    kind = grad_out.dtype
    pair = pltpu.SemaphoreType.DMA((2, 2))
    eight = pltpu.SemaphoreType.DMA((2 * LINE,))
    four = pltpu.SemaphoreType.DMA((4,))
    one = pltpu.SemaphoreType.DMA
    return pl.pallas_call(
        kernel,
        out_shape=(
            jax.ShapeDtypeStruct((tokens, hidden), kind),
            jax.ShapeDtypeStruct((tokens * LINE, features), kind),
        ),
        in_specs=[pl.BlockSpec(memory_space=pltpu.HBM)] * 3,
        out_specs=(pl.BlockSpec(memory_space=pltpu.HBM),) * 2,
        scratch_shapes=[
            pltpu.VMEM((2, TILES, width // TILES, features), kind),
            pltpu.VMEM((2 * rows, features), kind),
            pltpu.VMEM((2 * LINE, 2, rows, width), kind),
            pltpu.VMEM((2, 2, rows, width), kind),
            pltpu.VMEM((4, rows, width), kind),
            pltpu.VMEM((2, 2, rows, width), kind),
            pltpu.SemaphoreType.DMA((2, TILES)),
            one, one, pair, pair, eight, eight, eight,
            pair, pair, four, four, four, pair,
        ],
        compiler_params=pltpu.CompilerParams(
            collective_id=0, has_side_effects=True, vmem_limit_bytes=63 * 1024 * 1024
        ),
        cost_estimate=pl.CostEstimate(
            flops=2 * LINE * tokens * hidden * features * 3,
            bytes_accessed=2 * (hidden * features + 12 * tokens * features),
            transcendentals=0,
        ),
    )(grad_out, down_weight, slope)


def fused_device(grad_out, preact, down_weight, sketch_matrix):
    value, slope = gelu_parts(preact)
    grad_pre, grad_rows = gathered_product(grad_out, down_weight, slope.astype(jnp.bfloat16))
    own = lax.dot_general(
        sketch_matrix, value.astype(jnp.bfloat16), (((0,), (1,)), ((), ())), preferred_element_type=jnp.float32
    )
    reduced = lax.psum_scatter(own.astype(jnp.bfloat16), "row", scatter_dimension=0, tiled=True)
    reduced = lax.all_gather(reduced.astype(jnp.bfloat16), "col", axis=1, tiled=True)
    sketch = jnp.dot(reduced, grad_rows, preferred_element_type=jnp.float32)
    return (grad_pre, sketch)


def solution(mesh):
    body = fused_device if fits(mesh) else per_device
    in_specs = (
        P(("groups", "row"), "col"),
        P(("groups", "col"), "row"),
        P("row", "col"),
        P("row", None),
    )
    out_specs = (P(("groups", "col"), "row"), P(("groups", "row"), "col"))
    return jax.shard_map(
        body, mesh=mesh, in_specs=in_specs, out_specs=out_specs, check_vma=False
    )
```

```python
import jax
import jax.numpy as jnp
from jax import lax
from jax.experimental import pallas as pl
from jax.experimental.pallas import tpu as pltpu
from jax.sharding import PartitionSpec as P

gelu_scale = 0.7978845608028654
cubic_term = 0.044715


def gelu_parts(preact):
    pre_f32 = preact.astype(jnp.float32)
    inner_arg = gelu_scale * (pre_f32 + cubic_term * pre_f32 * pre_f32 * pre_f32)
    tangent = jnp.tanh(inner_arg)
    value = 0.5 * pre_f32 * (1.0 + tangent)
    slope = 0.5 * (1.0 + tangent) + 0.5 * pre_f32 * (1.0 - tangent * tangent) * gelu_scale * (
        1.0 + 3.0 * cubic_term * pre_f32 * pre_f32
    )
    return (value, slope)


def per_device(grad_out, preact, down_weight, sketch_matrix):
    grad_rows = lax.all_gather(grad_out, "row", axis=0, tiled=True)
    value, slope = gelu_parts(preact)
    act_local = value.astype(jnp.bfloat16)
    own = lax.dot_general(
        sketch_matrix, act_local, (((0,), (1,)), ((), ())), preferred_element_type=jnp.float32
    )
    reduced = lax.psum_scatter(own, "row", scatter_dimension=0, tiled=True)
    reduced = lax.all_gather(reduced.astype(jnp.bfloat16), "col", axis=1, tiled=True)
    hidden_grad = lax.psum_scatter(
        lax.dot_general(
            grad_rows, down_weight, (((1,), (1,)), ((), ())), preferred_element_type=jnp.float32
        ).astype(jnp.bfloat16),
        "col",
        scatter_dimension=0,
        tiled=True,
    ).astype(jnp.float32)
    grad_pre = (hidden_grad * slope).astype(jnp.bfloat16)
    sketch = jnp.dot(reduced, grad_rows, preferred_element_type=jnp.float32)
    return (grad_pre, sketch)


MESH = pl.DeviceIdType.MESH
LINE = 4
TILES = 4


def fits(mesh):
    return mesh.shape["row"] == LINE and mesh.shape["col"] == LINE


def pick(index, options):
    chosen = options[0]
    for place, option in enumerate(options[1:], 1):
        chosen = jnp.where(index == place, option, chosen)
    return chosen


def arrival_orders():
    codes = []
    for place in range(LINE):
        order = sorted(range(LINE), key=lambda block: (abs(block - place), block))
        codes.append(sum(block * LINE**position for position, block in enumerate(order)))
    return codes


def kernel(
    g_ref, w_ref, slope_ref, out_ref, rows_ref,
    wbuf, gbuf, pbuf, near, far, sums,
    w_sem, g_sem, own_sem, slope_sem, out_sem, right_sem, left_sem, got_sem,
    near_send, near_got, far_send, far_got, sum_send, sum_got,
):
    z = lax.axis_index("row")
    c = lax.axis_index("col")
    par = lax.rem(c, 2)
    other = 1 - par
    partner = c + 1 - 2 * par
    chip = lax.div(c, 2)
    has_left, has_right = z > 0, z < LINE - 1
    piece_rows = gbuf.shape[0] // 2
    tile = wbuf.shape[2]
    half_width = tile * TILES

    def w_copy(half, j):
        start = pl.multiple_of((half * TILES + j) * tile, tile)
        return pltpu.make_async_copy(w_ref.at[pl.ds(start, tile)], wbuf.at[half, j], w_sem.at[half, j])

    def slope_copy(h, half):
        return pltpu.make_async_copy(
            slope_ref.at[pl.ds(h * piece_rows, piece_rows), pl.ds(half * half_width, half_width)],
            far.at[2 * h + half],
            slope_sem.at[h, half],
        )

    def out_copy(h, half):
        return pltpu.make_async_copy(
            pbuf.at[2 * c + h, half],
            out_ref.at[pl.ds(h * piece_rows, piece_rows), pl.ds(half * half_width, half_width)],
            out_sem.at[h, half],
        )

    def rows_of(piece):
        return rows_ref.at[pl.ds(pl.multiple_of(piece * piece_rows, piece_rows), piece_rows)]

    def own_copy():
        return pltpu.make_async_copy(
            g_ref, rows_ref.at[pl.ds(pl.multiple_of(z * 2 * piece_rows, 2 * piece_rows), 2 * piece_rows)], own_sem
        )

    def pass_on(piece, step, sem, source):
        return pltpu.make_async_remote_copy(
            src_ref=source, dst_ref=rows_of(piece), send_sem=sem.at[piece], recv_sem=got_sem.at[piece],
            device_id={"row": z + step}, device_id_type=MESH,
        )

    def near_copy(piece, h, half):
        return pltpu.make_async_remote_copy(
            src_ref=pbuf.at[piece, half], dst_ref=near.at[h, half],
            send_sem=near_send.at[h, half], recv_sem=near_got.at[h, half],
            device_id={"col": partner}, device_id_type=MESH,
        )

    def part(q):
        return pl.ds(q * (half_width // 2), half_width // 2)

    def far_copy(piece, index, q):
        return pltpu.make_async_remote_copy(
            src_ref=pbuf.at[piece, other, :, part(q)], dst_ref=far.at[index, :, part(q)],
            send_sem=far_send.at[index, q], recv_sem=far_got.at[index, q],
            device_id={"col": partner}, device_id_type=MESH,
        )

    def sum_copy(piece, owner, h, half, index, q):
        return pltpu.make_async_remote_copy(
            src_ref=pbuf.at[piece, half, :, part(q)], dst_ref=sums.at[h, half, :, part(q)],
            send_sem=sum_send.at[index, q], recv_sem=sum_got.at[h, half, q],
            device_id={"col": owner}, device_id_type=MESH,
        )

    own_copy().start()

    @pl.loop(0, TILES)
    def _(j):
        w_copy(other, j).start()

    barrier = pltpu.get_barrier_semaphore()
    for step in range(1, LINE):
        pl.semaphore_signal(barrier, inc=1, device_id={"col": lax.rem(c + step, LINE)}, device_id_type=MESH)

    @pl.when(has_left)
    def _():
        pl.semaphore_signal(barrier, inc=1, device_id={"row": z - 1}, device_id_type=MESH)

    @pl.when(has_right)
    def _():
        pl.semaphore_signal(barrier, inc=1, device_id={"row": z + 1}, device_id_type=MESH)

    pl.semaphore_wait(barrier, LINE - 1 + jnp.where(has_left, 1, 0) + jnp.where(has_right, 1, 0))

    for h in range(2):
        source = g_ref.at[pl.ds(h * piece_rows, piece_rows)]

        @pl.when(has_left)
        def _():
            pass_on(2 * z + h, -1, left_sem, source).start()

        @pl.when(has_right)
        def _():
            pass_on(2 * z + h, 1, right_sem, source).start()

    @pl.loop(0, TILES)
    def _(j):
        w_copy(par, j).start()

    own_copy().wait()

    def receive(block):
        for h in range(2):
            piece = 2 * block + h
            pass_on(piece, 0, left_sem, rows_of(piece)).wait_recv()

            @pl.when((block < z) & has_right)
            def _():
                pass_on(piece, 1, right_sem, rows_of(piece)).start()

            @pl.when((block > z) & has_left)
            def _():
                pass_on(piece, -1, left_sem, rows_of(piece)).start()

    middle = has_left & has_right

    def step_of(s, code):
        owner = lax.rem(code, LINE)
        later = lax.rem(lax.div(code, LINE), LINE)
        is_near = owner == partner
        is_far = lax.div(owner, 2) != chip
        first = 2 * lax.rem(owner, 2)

        @pl.when((s > 0) & ((s != 2) | jnp.logical_not(middle)))
        def _():
            receive(owner)

        @pl.when((s == 1) & middle)
        def _():
            receive(later)

        start = pl.multiple_of(owner * 2 * piece_rows, 2 * piece_rows)
        load = pltpu.make_async_copy(rows_ref.at[pl.ds(start, 2 * piece_rows)], gbuf, g_sem)
        load.start()
        load.wait()

        def multiply(half, q):
            @pl.loop(q * (TILES // 2), (q + 1) * (TILES // 2))
            def _(j):
                @pl.when(s == 0)
                def _():
                    w_copy(half, j).wait()

                product = lax.dot_general(
                    gbuf[...], wbuf[half, j], (((1,), (1,)), ((), ())), preferred_element_type=jnp.float32
                ).astype(jnp.bfloat16)
                columns = pl.ds(pl.multiple_of(j * tile, tile), tile)
                for h in range(2):
                    pbuf[2 * owner + h, half, :, columns] = product[h * piece_rows : (h + 1) * piece_rows]

        for q in range(2):
            multiply(other, q)

            @pl.when(is_far)
            def _():
                for h in range(2):
                    far_copy(2 * owner + h, first + h, q).start()

            multiply(par, q)

            @pl.when(is_far)
            def _():
                for h in range(2):
                    piece, index = 2 * owner + h, first + h
                    far_copy(piece, index, q).wait_recv()

                    @pl.loop(q * (TILES // 2), (q + 1) * (TILES // 2))
                    def _(j):
                        columns = pl.ds(pl.multiple_of(j * tile, tile), tile)
                        total = pbuf[piece, par, :, columns].astype(jnp.float32) + far[index, :, columns].astype(
                            jnp.float32
                        )
                        pbuf[piece, par, :, columns] = total.astype(jnp.bfloat16)

                    sum_copy(piece, owner, h, par, index, q).start()

        @pl.when(is_near)
        def _():
            for half in range(2):
                for h in range(2):
                    near_copy(2 * owner + h, h, half).start()

        return lax.div(code, LINE)

    lax.fori_loop(0, LINE, step_of, pick(z, arrival_orders()))

    for h in range(2):
        for half in range(2):
            slope_copy(h, half).start()

    for h in range(2):
        for half in range(2):
            near_copy(2 * partner + h, h, half).wait_recv()
            slope_copy(h, half).wait()
            for q in range(2):
                sum_copy(2 * c + h, lax.rem(c + 2, LINE), h, half, h, q).wait_recv()

            @pl.loop(0, TILES)
            def _(j):
                columns = pl.ds(pl.multiple_of(j * tile, tile), tile)
                hidden = (
                    pbuf[2 * c + h, half, :, columns].astype(jnp.float32)
                    + near[h, half, :, columns].astype(jnp.float32)
                    + sums[h, half, :, columns].astype(jnp.float32)
                )
                scaled = hidden * far[2 * h + half, :, columns].astype(jnp.float32)
                pbuf[2 * c + h, half, :, columns] = scaled.astype(jnp.bfloat16)

            out_copy(h, half).start()

    def drain(piece, carry):
        owner = lax.div(piece, 2)
        h = lax.rem(piece, 2)
        index = 2 * lax.rem(owner, 2) + h

        @pl.when((owner <= z) & has_right)
        def _():
            pass_on(piece, 1, right_sem, rows_of(piece)).wait_send()

        @pl.when((owner >= z) & has_left)
        def _():
            pass_on(piece, -1, left_sem, rows_of(piece)).wait_send()

        @pl.when(owner == partner)
        def _():
            near_copy(piece, h, other).wait_send()
            near_copy(piece, h, par).wait_send()

        @pl.when(lax.div(owner, 2) != chip)
        def _():
            for q in range(2):
                far_copy(piece, index, q).wait_send()
                sum_copy(piece, owner, h, par, index, q).wait_send()

        return carry

    lax.fori_loop(0, 2 * LINE, drain, 0)
    for h in range(2):
        for half in range(2):
            out_copy(h, half).wait()


def gathered_product(grad_out, down_weight, slope):
    tokens, features = grad_out.shape
    hidden = down_weight.shape[0]
    rows, width = tokens // 2, hidden // 2
    kind = grad_out.dtype
    pair = pltpu.SemaphoreType.DMA((2, 2))
    eight = pltpu.SemaphoreType.DMA((2 * LINE,))
    four = pltpu.SemaphoreType.DMA((4, 2))
    one = pltpu.SemaphoreType.DMA
    return pl.pallas_call(
        kernel,
        out_shape=(
            jax.ShapeDtypeStruct((tokens, hidden), kind),
            jax.ShapeDtypeStruct((tokens * LINE, features), kind),
        ),
        in_specs=[pl.BlockSpec(memory_space=pltpu.HBM)] * 3,
        out_specs=(pl.BlockSpec(memory_space=pltpu.HBM),) * 2,
        scratch_shapes=[
            pltpu.VMEM((2, TILES, width // TILES, features), kind),
            pltpu.VMEM((2 * rows, features), kind),
            pltpu.VMEM((2 * LINE, 2, rows, width), kind),
            pltpu.VMEM((2, 2, rows, width), kind),
            pltpu.VMEM((4, rows, width), kind),
            pltpu.VMEM((2, 2, rows, width), kind),
            pltpu.SemaphoreType.DMA((2, TILES)),
            one, one, pair, pair, eight, eight, eight,
            pair, pair, four, four, four, pltpu.SemaphoreType.DMA((2, 2, 2)),
        ],
        compiler_params=pltpu.CompilerParams(
            collective_id=0, has_side_effects=True, vmem_limit_bytes=63 * 1024 * 1024
        ),
        cost_estimate=pl.CostEstimate(
            flops=2 * LINE * tokens * hidden * features * 3,
            bytes_accessed=2 * (hidden * features + 12 * tokens * features),
            transcendentals=0,
        ),
    )(grad_out, down_weight, slope)


def fused_device(grad_out, preact, down_weight, sketch_matrix):
    value, slope = gelu_parts(preact)
    grad_pre, grad_rows = gathered_product(grad_out, down_weight, slope.astype(jnp.bfloat16))
    own = lax.dot_general(
        sketch_matrix, value.astype(jnp.bfloat16), (((0,), (1,)), ((), ())), preferred_element_type=jnp.float32
    )
    reduced = lax.psum_scatter(own.astype(jnp.bfloat16), "row", scatter_dimension=0, tiled=True)
    reduced = lax.all_gather(reduced.astype(jnp.bfloat16), "col", axis=1, tiled=True)
    sketch = jnp.dot(reduced, grad_rows, preferred_element_type=jnp.float32)
    return (grad_pre, sketch)


def solution(mesh):
    body = fused_device if fits(mesh) else per_device
    in_specs = (
        P(("groups", "row"), "col"),
        P(("groups", "col"), "row"),
        P("row", "col"),
        P("row", None),
    )
    out_specs = (P(("groups", "col"), "row"), P(("groups", "row"), "col"))
    return jax.shard_map(
        body, mesh=mesh, in_specs=in_specs, out_specs=out_specs, check_vma=False
    )
```
